512 devices in a mesh: dp: 32 (over x_hi, y, core), seq: 16 (over x_lo, z).
Axes of the slice: x: 4 (x_hi: 2, x_lo: 2; x = x_hi * 2 + x_lo), y: 8, z: 8, core: 2. Of those that a mesh axis runs over, the one named last changes fastest.
Arguments:
- query: bfloat16 [32, 2048, 4096], P('dp', 'seq'), may hold values from -108 to 108
- keys: bfloat16 [32, 2048, 512], P('dp', 'seq'), may hold values from -9 to 9
- values: bfloat16 [32, 2048, 512], P('dp', 'seq'), may hold values from -6 to 6
- grad_out: bfloat16 [32, 2048, 4096], P('dp', 'seq'), may hold values from -6 to 6
- positions: int32 [32, 2048], P('dp', 'seq'), may hold values from 0 to 16383, as said below
- q_scale: float32 [4096], replicated, may hold values from 0.1 to 1.9
- k_scale: float32 [512], replicated, may hold values from 0.1 to 1.9
Outputs:
- grad_query: bfloat16 [32, 2048, 4096], P('dp', 'seq')
- grad_keys: bfloat16 [32, 2048, 512], P('dp', 'seq')
- grad_values: bfloat16 [32, 2048, 512], P('dp', 'seq')
- grad_qscale: float32 [4096], replicated
- grad_kscale: float32 [512], replicated
The draws below stay inside these ranges and needn't reach their ends.
Inputs may be any that keep to these rules, and one draw needn't show every extreme that they name: Along each sequence positions rise by 1 or 2 from one token to the next; some sequence ends at position 16383.
All inputs are finite; a program needn't handle non-finite values.
Results may differ from the reference program's by a relative error of at most 0.035.
Values may be sent and summed in bfloat16 or wider, within the bound.
No kernel may reach another device: no remote copies, remote signals or barrier semaphores. Data moves between devices by JAX's collectives and lax.ppermute only.
A program may use at most 128 MiB of HBM per device.

```python
import math
import jax
import jax.numpy as jnp
from jax import lax

HQ = 32
HK = 4
HD = 128
CONTEXT = 16384
LENGTH = 2048
SEQS = 32


def base_keys(key):
    raw = jax.random.normal(jax.random.fold_in(key, 11), (SEQS, LENGTH, HK, HD), jnp.float32)
    return jnp.clip(raw, -6.0, 6.0)


def draw_keys(key, part):
    shared = base_keys(key)
    return shared.reshape(SEQS, LENGTH, HK * HD).astype(jnp.bfloat16)


def draw_query(key, part):
    key = jax.random.fold_in(key, 2)
    raw = jnp.clip(jax.random.normal(key, (SEQS, LENGTH, HQ, HD), jnp.float32), -6.0, 6.0)
    return raw.reshape(SEQS, LENGTH, HQ * HD).astype(jnp.bfloat16)


def draw_positions(key, part):
    key = jax.random.fold_in(key, 3)
    gaps = jax.random.randint(jax.random.fold_in(key, 5), (SEQS, LENGTH), 0, 2)
    gaps = jnp.where(jnp.arange(LENGTH)[None, :] == 0, 0, gaps)
    offsets = jnp.cumsum(gaps + 1, axis=1) - 1
    last = offsets[:, -1]
    starts = jax.random.randint(key, (SEQS,), 0, CONTEXT - 2 * LENGTH + 2)
    chosen = jax.random.randint(jax.random.fold_in(key, 4), (), 0, SEQS)
    starts = jnp.where(jnp.arange(SEQS) == chosen, CONTEXT - 1 - last, starts)
    return (starts[:, None] + offsets).astype(jnp.int32)


def level_of(rng, dims, cuts, low, top_value):
    def one(axis_at, parts):
        heights = jax.random.uniform(jax.random.fold_in(jax.random.fold_in(rng, 6), axis_at), (parts,), jnp.float32, low / len(cuts), top_value / len(cuts))
        return jnp.repeat(jnp.exp(heights), dims[axis_at] // parts).reshape((-1,) + (1,) * (len(dims) - axis_at - 1))

    level = one(*cuts[0])
    for cut in cuts[1:]:
        level = level * one(*cut)
    return level


def scatter_about(stream_key, shape, deviation, limit, cuts=(), kind=jnp.bfloat16):
    drawn = deviation * jax.random.normal(stream_key, shape, jnp.float32)
    if cuts:
        drawn = drawn * level_of(stream_key, shape, cuts, -0.22, 0.18)
    return jnp.clip(drawn, -limit, limit).astype(kind)


def setup_inputs(seed: int = 0) -> dict:
    streams_of = jax.random.split(jax.random.key(seed), 8)
    return {
        "query": draw_query(jax.random.fold_in(streams_of[7], 71), 0),
        "keys": draw_keys(jax.random.fold_in(streams_of[7], 71), 0),
        "values": scatter_about(streams_of[2], (SEQS, LENGTH, HK * HD), 1.0, 6.0, ((0, 32), (1, 16))),
        "grad_out": scatter_about(streams_of[3], (SEQS, LENGTH, HQ * HD), 1.0, 6.0, ((0, 32), (1, 16))),
        "positions": draw_positions(jax.random.fold_in(streams_of[7], 71), 0),
        "q_scale": jnp.clip(1.0 + 0.18 * jax.random.normal(streams_of[5], (HQ * HD,), jnp.float32), 0.1, 1.9),
        "k_scale": jnp.clip(1.0 + 0.18 * jax.random.normal(streams_of[6], (HK * HD,), jnp.float32), 0.1, 1.9),
    }


rope_base = 1000000.0

def angles(pos, width):
    half = width // 2
    freq = rope_base ** (-(jnp.arange(half, dtype=jnp.float32) * 2.0) / width)
    angle = pos.astype(jnp.float32)[..., None] * freq
    return (jnp.cos(angle)[..., None, :], jnp.sin(angle)[..., None, :])

def rotate(inputs, pos):
    half = inputs.shape[-1] // 2
    cosine, sine = angles(pos, inputs.shape[-1])
    first = inputs[..., :half]
    second = inputs[..., half:]
    return jnp.concatenate([first * cosine - second * sine, second * cosine + first * sine], axis=-1)

def unrotate(grads, pos):
    half = grads.shape[-1] // 2
    cosine, sine = angles(pos, grads.shape[-1])
    first = grads[..., :half]
    second = grads[..., half:]
    return jnp.concatenate([first * cosine + second * sine, second * cosine - first * sine], axis=-1)

def rounded(values_in):
    return lax.optimization_barrier(values_in.astype(jnp.bfloat16)).astype(jnp.float32)

def reference(query, keys, values, grad_out, positions, q_scale, k_scale):
    group = HQ // HK
    q_gain = q_scale.reshape(HQ, HD)
    k_gain = k_scale.reshape(HK, HD)
    block = math.gcd(LENGTH, 256)
    factor = 1.0 / math.sqrt(HD)

    def one_sequence(items):
        q_in, k_in, v_in, d_in, pos = items
        q_raw = q_in.reshape(LENGTH, HQ, HD).astype(jnp.float32)
        k_raw = k_in.reshape(LENGTH, HK, HD).astype(jnp.float32)
        q_rot = rounded(rotate(q_raw * q_gain, pos))
        k_rot = rounded(rotate(k_raw * k_gain, pos))
        q_heads = jnp.transpose(q_rot, (1, 0, 2))
        k_heads = jnp.repeat(jnp.transpose(k_rot, (1, 0, 2)), group, axis=0)
        v_heads = jnp.repeat(jnp.transpose(v_in.reshape(LENGTH, HK, HD), (1, 0, 2)), group, axis=0).astype(jnp.float32)
        d_heads = jnp.transpose(d_in.reshape(LENGTH, HQ, HD), (1, 0, 2)).astype(jnp.float32)
        grad_k = jnp.zeros((HQ, LENGTH, HD), jnp.float32)
        grad_v = jnp.zeros((HQ, LENGTH, HD), jnp.float32)
        pieces = []
        for start in range(0, LENGTH, block):
            end = start + block
            q_blk = q_heads[:, start:end]
            d_blk = d_heads[:, start:end]
            k_blk = k_heads[:, :end]
            v_blk = v_heads[:, :end]
            scores = jnp.einsum('hqd,hkd->hqk', q_blk, k_blk) * factor
            rows = start + jnp.arange(block)[:, None]
            cols = jnp.arange(end)[None, :]
            scores = jnp.where((cols <= rows)[None], scores, -jnp.inf)
            top = lax.optimization_barrier(jnp.max(scores, axis=-1, keepdims=True))
            weights = jnp.exp(scores - top)
            probs = weights / lax.optimization_barrier(jnp.sum(weights, axis=-1, keepdims=True))
            probs_b = rounded(probs)
            attended = jnp.einsum('hqk,hkd->hqd', probs_b, v_blk)
            delta = lax.optimization_barrier(jnp.sum(d_blk * attended, axis=-1))
            dprob = jnp.einsum('hqd,hkd->hqk', d_blk, v_blk)
            dscore = rounded(probs * (dprob - delta[:, :, None]) * factor)
            pieces.append(jnp.einsum('hqk,hkd->hqd', dscore, k_blk).astype(jnp.bfloat16))
            grad_k = grad_k.at[:, :end].add(jnp.einsum('hqk,hqd->hkd', dscore, q_blk))
            grad_v = grad_v.at[:, :end].add(jnp.einsum('hqk,hqd->hkd', probs_b, d_blk))
        dq_rot = lax.optimization_barrier(jnp.transpose(jnp.concatenate(pieces, axis=1), (1, 0, 2))).astype(jnp.float32)
        dk_sum = jnp.transpose(grad_k, (1, 0, 2)).reshape(LENGTH, HK, group, HD).sum(axis=2)
        dv_sum = jnp.transpose(grad_v, (1, 0, 2)).reshape(LENGTH, HK, group, HD).sum(axis=2)
        dk_rot = rounded(dk_sum)
        back_q = unrotate(dq_rot, pos)
        back_k = unrotate(dk_rot, pos)
        return ((back_q * q_gain).astype(jnp.bfloat16).reshape(LENGTH, HQ * HD), (back_k * k_gain).astype(jnp.bfloat16).reshape(LENGTH, HK * HD), dv_sum.astype(jnp.bfloat16).reshape(LENGTH, HK * HD), lax.optimization_barrier(jnp.sum(q_raw * back_q, axis=0)).reshape(HQ * HD), lax.optimization_barrier(jnp.sum(k_raw * back_k, axis=0)).reshape(HK * HD))
    results = lax.map(one_sequence, (query, keys, values, grad_out, positions))
    return (results[0], results[1], results[2], lax.optimization_barrier(jnp.sum(results[3], axis=0)), lax.optimization_barrier(jnp.sum(results[4], axis=0)))
```

```python
import math

import jax
import jax.numpy as jnp
from jax import lax
from jax.experimental import pallas as pl
from jax.experimental.pallas import tpu as pltpu
from jax.sharding import PartitionSpec as P

HQ = 32
HK = 4
HD = 128
BLK = 128
EXTRA = 16
SUB = 4
ROWS = 2 * SUB * BLK
CHUNK = 256
KEYS = 512
FACTOR = 1.0 / math.sqrt(HD)
EXP2 = FACTOR * math.log2(math.e)
NEG = -1e30
rope_base = 1000000.0

f32 = jnp.float32
bf16 = jnp.bfloat16
VMEM = pl.BlockSpec(memory_space=pltpu.VMEM)
SMEM = pl.BlockSpec(memory_space=pltpu.SMEM)
ANY = pl.BlockSpec(memory_space=pl.ANY)


def shape(dims, dtype):
    return jax.ShapeDtypeStruct(dims, dtype)


def params(mib):
    return pltpu.CompilerParams(vmem_limit_bytes=mib << 20)


def turn(x, c, s):
    return x * c + pltpu.roll(x, HD // 2, 1) * s


def unturn(x, c, s):
    return x * c - pltpu.roll(x, HD // 2, 1) * s


def two_parts(x):
    high = lax.reduce_precision(x, 8, 7)
    return jnp.concatenate([high, x - high], axis=-1).astype(bf16)


def angle_tables():
    half = HD // 2
    freq = rope_base ** (-(jnp.arange(half, dtype=f32) * 2.0) / HD)
    freq = jnp.concatenate([freq, freq])[None]
    steps = jnp.arange(BLK, dtype=f32)[:, None]
    out = []
    for angle in (steps * BLK * freq, steps * freq):
        out.append(two_parts(jnp.concatenate([jnp.cos(angle), jnp.sin(angle)], axis=-1)))
    return jnp.stack(out)


def full_table(pos):
    half = HD // 2
    freq = rope_base ** (-(jnp.arange(half, dtype=f32) * 2.0) / HD)
    angle = pos.astype(f32)[:, None] * freq
    cosine, sine = jnp.cos(angle), jnp.sin(angle)
    return jnp.concatenate([cosine, cosine, -sine, sine], axis=-1)


def pack_kernel(place_ref, q_ref, d_ref, k_ref, v_ref, pos_ref, *outs):
    own_ref, x_ref, za_ref, da_ref, zb_ref, db_ref, kv_ref = outs
    mine = place_ref[0]

    def put(out, head, sub):
        for which, ref in enumerate((q_ref, d_ref)):
            for h in range(SUB):
                at = pl.multiple_of(((head * 2 + sub) * SUB + h) * HD, HD)
                out[which, h] = ref[:, pl.ds(at, HD)]

    for sub in range(2):
        put(own_ref.at[sub], mine, sub)
        put(x_ref.at[sub], mine ^ 2, sub)
    put(za_ref, mine ^ 1, 0)
    put(da_ref, mine ^ 3, 0)
    put(zb_ref, mine ^ 1, 1)
    put(db_ref, mine ^ 3, 1)
    pos = pos_ref[...]
    high = jnp.broadcast_to((pos >> 7).astype(f32), (EXTRA, BLK)).astype(bf16)
    low = jnp.broadcast_to((pos & 127).astype(f32), (EXTRA, BLK)).astype(bf16)
    n = kv_ref.shape[0]
    for i in range(n):
        head = (i // (n // 2)) * 2 + i % 2
        cols = slice(head * HD, (head + 1) * HD)
        kv_ref[i, :BLK, :HD] = k_ref[:, cols]
        kv_ref[i, :BLK, HD:] = v_ref[:, cols]
        kv_ref[i, BLK:, :HD] = high
        kv_ref[i, BLK:, HD:] = low


def pack(place, query, grad_out, keys, values, positions, n):
    one = shape((2, SUB, BLK, HD), bf16)
    both = shape((2, 2, SUB, BLK, HD), bf16)
    return pl.pallas_call(
        pack_kernel,
        out_shape=(both, both, one, one, one, one, shape((n, BLK + EXTRA, 2 * HD), bf16)),
        in_specs=[SMEM] + [VMEM] * 5,
        out_specs=(VMEM,) * 7,
        compiler_params=params(24),
        cost_estimate=pl.CostEstimate(flops=0, bytes_accessed=6 << 20, transcendentals=0),
        name="pack",
    )(place, query, grad_out, keys, values, positions)


def attend_kernel(
    blocks_ref, own_ref, x_ref, za_ref, da_ref, zb_ref, db_ref, kv_hbm, table_ref, ks_ref, qs_ref,
    go_ref, gx_ref, gza_ref, gda_ref, gzb_ref, gdb_ref, term_ref, dkv_ref,
    s_scr, p_scr, qd_scr, kv_ref, cs_ref, kr_ref, kt_ref, q_scr, qt_scr, dt_scr, dq_scr, m_scr, l_scr, e_scr,
    gq_scr, dk_ref, dv_ref, tq_ref, sems, kv_sem,
):
    n = kv_ref.shape[0]
    kv_copy = pltpu.make_async_copy(kv_hbm, kv_ref, kv_sem)
    kv_copy.start()
    first, second = pl.ds(0, SUB), pl.ds(SUB, SUB)
    copies = [
        pltpu.make_async_copy(src, qd_scr.at[u, :, heads], sems.at[i])
        for i, (src, u, heads) in enumerate((
            (own_ref.at[0], 0, first), (own_ref.at[1], 0, second),
            (x_ref.at[0], 1, first), (x_ref.at[1], 1, second),
            (za_ref, 2, first), (zb_ref, 2, second),
            (da_ref, 3, first), (db_ref, 3, second),
        ))
    ]
    for copy in copies:
        copy.start()
    dk_ref[...] = jnp.zeros_like(dk_ref)
    dv_ref[...] = jnp.zeros_like(dv_ref)
    tq_ref[...] = jnp.zeros_like(tq_ref)
    sign = jnp.where(lax.broadcasted_iota(jnp.int32, (BLK, HD), 1) < HD // 2, -1.0, 1.0)
    row = lax.broadcasted_iota(jnp.int32, (BLK, BLK), 0).astype(f32)
    kv_copy.wait()

    def pick(i, part):
        pos = kv_ref[i, BLK : BLK + EXTRA, part * HD : (part + 1) * HD].astype(f32)[:1]
        hot = jnp.where(row == pos, 1.0, 0.0).T.astype(bf16)
        got = jnp.dot(hot, table_ref[part], preferred_element_type=f32)
        got = got[:, : 2 * HD] + got[:, 2 * HD :]
        return got[:, :HD], got[:, HD:]

    per = KEYS // BLK

    def ready(w, carry):
        for j in range(per):
            i = w * per + j
            at = pl.ds(pl.multiple_of(i * BLK, BLK), BLK)
            ch, sh = pick(i, 0)
            cl, sl = pick(i, 1)
            c = ch * cl - sh * sl
            s = (sh * cl + ch * sl) * sign
            cs_ref[at, :HD] = c
            cs_ref[at, HD:] = s
            r = turn(kv_ref[i, :BLK, :HD].astype(f32) * ks_ref[...], c, s)
            kr_ref[at, :] = r.astype(bf16)
            kt_ref[w, :, j * BLK : (j + 1) * BLK] = r.T.astype(bf16)
        return carry

    lax.fori_loop(0, n // per, ready, 0)
    for copy in copies:
        copy.wait()
    sub8 = lax.broadcasted_iota(jnp.int32, (8, ROWS), 0)
    lane = lax.broadcasted_iota(jnp.int32, (8, ROWS), 1)
    group = lax.broadcasted_iota(jnp.int32, (CHUNK // 8, 8, ROWS), 0) * 8

    def unit(u, carry):
        b0, b1 = blocks_ref[2 * u], blocks_ref[2 * u + 1]
        tabs = []
        for b in (b0, b1):
            toks = pl.ds(pl.multiple_of(b * BLK, BLK), BLK)
            tabs.append((cs_ref[toks, :HD], cs_ref[toks, HD:]))
        for h in range(2 * SUB):
            cols = slice(h * BLK, (h + 1) * BLK)
            r = turn(qd_scr[u, 0, h].astype(f32) * qs_ref[h : h + 1, :], *tabs[h // SUB])
            q_scr[cols, :] = r.astype(bf16)
            qt_scr[:, cols] = r.T.astype(bf16)
            dt_scr[:, cols] = qd_scr[u, 1, h].astype(f32).T.astype(bf16)
        dq_scr[...] = jnp.zeros_like(dq_scr)
        token = jnp.where(lane < ROWS // 2, b0, b1) * BLK + (lane & (BLK - 1)) - sub8
        steps = jnp.maximum(b0, b1) // per + 1

        def look(w, stats):
            m, l, d = stats
            for j in range(KEYS // CHUNK):
                at = pl.ds(pl.multiple_of(w * KEYS + j * CHUNK, CHUNK), CHUNK)
                vals = kv_ref[pl.ds(w * per + j * (CHUNK // BLK), CHUNK // BLK), :BLK, HD:]
                s = jnp.dot(kr_ref[at, :], qt_scr[...], preferred_element_type=f32)
                dp = jnp.dot(vals.reshape(CHUNK, HD), dt_scr[...], preferred_element_type=f32)
                p_scr[at, :] = dp
                s3 = s.reshape(CHUNK // 8, 8, ROWS)
                dp3 = dp.reshape(CHUNK // 8, 8, ROWS)
                s3 = jnp.where(group <= (token - (w * KEYS + j * CHUNK))[None], s3, NEG)
                s_scr[at, :] = s3.reshape(CHUNK, ROWS)
                mn = jnp.maximum(m, jnp.max(s3, axis=0))
                a = jnp.exp2((m - mn) * EXP2)
                e = jnp.exp2((s3 - mn[None]) * EXP2)
                m, l, d = mn, l * a + jnp.sum(e, axis=0), d * a + jnp.sum(e * dp3, axis=0)
            return m, l, d

        zero = jnp.zeros((8, ROWS), f32)
        m, l, d = lax.fori_loop(0, steps, look, (zero + NEG, zero, zero))
        top = jnp.max(m, axis=0, keepdims=True)
        w = jnp.exp2((m - top) * EXP2)
        total = jnp.sum(l * w, axis=0, keepdims=True)
        delta = jnp.sum(d * w, axis=0, keepdims=True) / total
        shift = top * EXP2 + jnp.log2(total)
        m_scr[...] = jnp.broadcast_to(shift, m_scr.shape)
        e_scr[...] = jnp.broadcast_to(delta, e_scr.shape)

        def back(w, carry):
            shift, delta = m_scr[...][None], e_scr[...][None]
            dq = dq_scr[...]
            for j in range(KEYS // CHUNK):
                at = pl.ds(pl.multiple_of(w * KEYS + j * CHUNK, CHUNK), CHUNK)
                s3 = s_scr[at, :].reshape(CHUNK // 8, 8, ROWS)
                dp3 = p_scr[at, :].reshape(CHUNK // 8, 8, ROWS)
                p = jnp.exp2(s3 * EXP2 - shift)
                ds = (p * (dp3 - delta)).reshape(CHUNK, ROWS).astype(bf16)
                p = p.reshape(CHUNK, ROWS).astype(bf16)
                dv_ref[at, :] += jnp.dot(p, qd_scr[u, 1].reshape(ROWS, HD), preferred_element_type=f32)
                dk_ref[at, :] += jnp.dot(ds, q_scr[...], preferred_element_type=f32)
                dq = dq + jnp.dot(
                    kt_ref[w, :, j * CHUNK : (j + 1) * CHUNK], ds, preferred_element_type=f32
                )
            dq_scr[...] = dq
            return carry

        lax.fori_loop(0, steps, back, 0)

        for h in range(2 * SUB):
            cos, sin = tabs[h // SUB]
            g = (dq_scr[:, h * BLK : (h + 1) * BLK] * FACTOR).T.astype(bf16).astype(f32)
            g = unturn(g, cos, sin)
            gq_scr[u, h] = (g * qs_ref[h : h + 1, :]).astype(bf16)
            tq_ref[h : h + 1, :] += jnp.sum(g * qd_scr[u, 0, h].astype(f32), axis=0, keepdims=True)
        return carry

    lax.fori_loop(0, 4, unit, 0)
    copies = [
        pltpu.make_async_copy(gq_scr.at[u, heads], dst, sems.at[i])
        for i, (dst, u, heads) in enumerate((
            (go_ref.at[0], 0, first), (go_ref.at[1], 0, second),
            (gx_ref.at[0], 1, first), (gx_ref.at[1], 1, second),
            (gza_ref, 2, first), (gzb_ref, 2, second),
            (gda_ref, 3, first), (gdb_ref, 3, second),
        ))
    ]
    for copy in copies:
        copy.start()

    def finish(c, tk):
        at = pl.ds(pl.multiple_of(c * BLK, BLK), BLK)
        g = dk_ref[at, :] * FACTOR
        dkv_ref[c, :BLK, :HD] = g.astype(bf16)
        dkv_ref[c, :BLK, HD:] = dv_ref[at, :].astype(bf16)
        dkv_ref[c, BLK:, :] = jnp.zeros((EXTRA, 2 * HD), bf16)
        g = unturn(g, cs_ref[at, :HD], cs_ref[at, HD:])
        return tk + jnp.sum(g * kv_ref[c, :BLK, :HD].astype(f32), axis=0, keepdims=True)

    tk = lax.fori_loop(0, n, finish, jnp.zeros((1, HD), f32))
    terms = jnp.concatenate([tq_ref[...], jnp.broadcast_to(tk, (8, HD))], axis=0)
    for j in range(term_ref.shape[0]):
        term_ref[j] = terms
    for copy in copies:
        copy.wait()


def attend(blocks, parts, kv, table, ks, qs, copies_of_term):
    n = kv.shape[0]
    length = n * BLK
    one, both = shape((SUB, BLK, HD), bf16), shape((2, SUB, BLK, HD), bf16)
    pairs = 4 * ROWS * length // 2
    return pl.pallas_call(
        attend_kernel,
        out_shape=(
            both, both, one, one, one, one,
            shape((copies_of_term, 2 * SUB + 8, HD), f32),
            shape(kv.shape, bf16),
        ),
        in_specs=[SMEM] + [ANY] * 7 + [VMEM] * 3,
        out_specs=(ANY,) * 6 + (VMEM,) * 2,
        scratch_shapes=[
            pltpu.VMEM((length, ROWS), f32),
            pltpu.VMEM((length, ROWS), f32),
            pltpu.VMEM((4, 2, 2 * SUB, BLK, HD), bf16),
            pltpu.VMEM(kv.shape, bf16),
            pltpu.VMEM((length, 2 * HD), f32),
            pltpu.VMEM((length, HD), bf16),
            pltpu.VMEM((length // KEYS, HD, KEYS), bf16),
            pltpu.VMEM((ROWS, HD), bf16),
            pltpu.VMEM((HD, ROWS), bf16),
            pltpu.VMEM((HD, ROWS), bf16),
            pltpu.VMEM((HD, ROWS), f32),
            pltpu.VMEM((8, ROWS), f32),
            pltpu.VMEM((8, ROWS), f32),
            pltpu.VMEM((8, ROWS), f32),
            pltpu.VMEM((4, 2 * SUB, BLK, HD), bf16),
            pltpu.VMEM((length, HD), f32),
            pltpu.VMEM((length, HD), f32),
            pltpu.VMEM((2 * SUB, HD), f32),
            pltpu.SemaphoreType.DMA((8,)),
            pltpu.SemaphoreType.DMA,
        ],
        compiler_params=params(44),
        cost_estimate=pl.CostEstimate(flops=pairs * HD * 20, bytes_accessed=8 << 20, transcendentals=pairs * 2),
        name="attend",
    )(blocks, *parts, kv, table, ks, qs)


def add_kernel(term_ref, dkv_in, dkv_ref, pair, sems):
    total = jnp.sum(term_ref[...], axis=0)
    high = total.astype(bf16)
    pair[:, :HD] = high
    pair[:, HD:] = (total - high.astype(f32)).astype(bf16)
    copies = [
        pltpu.make_async_copy(pair, dkv_ref.at[i, pl.ds(BLK, EXTRA)], sems.at[i])
        for i in range(dkv_ref.shape[0])
    ]
    for copy in copies:
        copy.start()
    for copy in copies:
        copy.wait()


def add(term, dkv):
    return pl.pallas_call(
        add_kernel,
        out_shape=shape(dkv.shape, bf16),
        in_specs=[VMEM, ANY],
        out_specs=ANY,
        scratch_shapes=[pltpu.VMEM((EXTRA, 2 * HD), bf16), pltpu.SemaphoreType.DMA((dkv.shape[0],))],
        input_output_aliases={1: 0},
        compiler_params=params(8),
        name="add",
    )(term, dkv)


def unpack_kernel(place_ref, own_ref, x_ref, za_ref, da_ref, zb_ref, db_ref, out_ref):
    mine = place_ref[0]

    def put(src, head, sub):
        for h in range(SUB):
            at = pl.multiple_of(((head * 2 + sub) * SUB + h) * HD, HD)
            out_ref[:, pl.ds(at, HD)] = src[h]

    for sub in range(2):
        put(own_ref.at[sub], mine, sub)
        put(x_ref.at[sub], mine ^ 2, sub)
    put(za_ref, mine ^ 1, 0)
    put(da_ref, mine ^ 3, 0)
    put(zb_ref, mine ^ 1, 1)
    put(db_ref, mine ^ 3, 1)


def unpack(place, parts):
    return pl.pallas_call(
        unpack_kernel,
        out_shape=shape((BLK, HQ * HD), bf16),
        in_specs=[SMEM] + [VMEM] * 6,
        out_specs=VMEM,
        compiler_params=params(8),
        cost_estimate=pl.CostEstimate(flops=0, bytes_accessed=2 << 20, transcendentals=0),
        name="unpack",
    )(place, *parts)


def final_kernel(dkv_ref, tab, ks_ref, gk_ref, gv_ref, tq_ref, tk_ref):
    n = dkv_ref.shape[0]
    for head in range(HK):
        first = (head // 2) * (n // 2) + head % 2
        got = jnp.zeros((BLK + EXTRA, 2 * HD), f32)
        for i in range(first, first + n // 2, 2):
            got = got + dkv_ref[i].astype(f32)
        cols = slice(head * HD, (head + 1) * HD)
        g = unturn(got[:BLK, :HD].astype(bf16).astype(f32), tab[:, :HD], tab[:, HD:])
        gk_ref[:, cols] = (g * ks_ref[head : head + 1, :]).astype(bf16)
        gv_ref[:, cols] = got[:BLK, HD:].astype(bf16)
        term = got[BLK:, :HD] + got[BLK:, HD:]
        tq_ref[head * 2 * SUB : (head + 1) * 2 * SUB, :] = term[: 2 * SUB]
        tk_ref[head : head + 1, :] = term[2 * SUB : 2 * SUB + 1]


def final(dkv, table, ks):
    return pl.pallas_call(
        final_kernel,
        out_shape=(
            shape((BLK, HK * HD), bf16),
            shape((BLK, HK * HD), bf16),
            shape((HQ, HD), f32),
            shape((HK, HD), f32),
        ),
        in_specs=[VMEM] * 3,
        out_specs=(VMEM,) * 4,
        compiler_params=params(8),
        name="final",
    )(dkv, table, ks)


def shards(query, keys, values, grad_out, positions, q_scale, k_scale):
    n = lax.axis_size("seq")
    half = n // 2
    me = lax.axis_index("seq")
    x, z = me // half, me % half
    odd = z % 2
    kind = x * 2 + odd
    place = jnp.stack([kind, me]).astype(jnp.int32)
    za = z + 1 - 2 * odd
    zb = (z - 1 + 2 * odd) % half

    def pairs(flip, step):
        out = []
        for i in range(n):
            xi, zi = i // half, i % half
            zo = (zi + step * (1 - 2 * (zi % 2))) % half
            out.append((i, (xi ^ flip) * half + zo))
        return out

    def send(a, flip, step):
        return lax.ppermute(a, "seq", pairs(flip, step))

    own, to_x, to_za, to_da, to_zb, to_db, kv = pack(
        place, query[0], grad_out[0], keys[0], values[0], positions, n
    )
    kv = lax.all_to_all(kv, "seq", 0, 0, tiled=True)
    in_x = send(to_x, 1, 0)
    in_za, in_da = send(to_za, 0, 1), send(to_da, 1, 1)
    in_zb, in_db = send(to_zb, 0, -1), send(to_db, 1, -1)

    q_gain = lax.dynamic_slice_in_dim(q_scale.reshape(HK, 2 * SUB, HD), kind, 1, 0)[0]
    k_gain = lax.dynamic_slice_in_dim(k_scale.reshape(HK, HD), kind, 1, 0)
    pair = lambda side: [side * half + za, side * half + zb]
    blocks = jnp.stack([me, me, me ^ half, me ^ half, *pair(x), *pair(1 - x)]).astype(jnp.int32)
    go, gx, gza, gda, gzb, gdb, term, dkv = attend(
        blocks,
        (own, in_x, in_za, in_da, in_zb, in_db),
        kv,
        angle_tables(),
        k_gain,
        q_gain,
        lax.axis_size("dp"),
    )

    term = lax.all_to_all(term, "dp", 0, 0, tiled=True)
    back = (go, send(gx, 1, 0), send(gza, 0, 1), send(gda, 1, 1), send(gzb, 0, -1), send(gdb, 1, -1))
    dkv, back = lax.optimization_barrier((add(term, dkv), back))
    dkv = lax.all_to_all(dkv, "seq", 0, 0, tiled=True)
    grad_query = unpack(place, back)
    grad_keys, grad_values, total_q, total_k = final(
        dkv, full_table(positions[0]), k_scale.reshape(HK, HD)
    )
    return (
        grad_query[None],
        grad_keys[None],
        grad_values[None],
        total_q.reshape(HQ * HD),
        total_k.reshape(HK * HD),
    )


def solution(mesh):
    return jax.shard_map(
        shards,
        mesh=mesh,
        in_specs=(
            P("dp", "seq", None),
            P("dp", "seq", None),
            P("dp", "seq", None),
            P("dp", "seq", None),
            P("dp", "seq"),
            P(),
            P(),
        ),
        out_specs=(P("dp", "seq", None), P("dp", "seq", None), P("dp", "seq", None), P(), P()),
        check_vma=False,
    )
```

```python
import math

import jax
import jax.numpy as jnp
from jax import lax
from jax.experimental import pallas as pl
from jax.experimental.pallas import tpu as pltpu
from jax.sharding import PartitionSpec as P

HQ = 32
HK = 4
HD = 128
BLK = 128
EXTRA = 16
SUB = 4
ROWS = 2 * SUB * BLK
CHUNK = 256
KEYS = 512
FACTOR = 1.0 / math.sqrt(HD)
EXP2 = FACTOR * math.log2(math.e)
NEG = -1e30
rope_base = 1000000.0

f32 = jnp.float32
bf16 = jnp.bfloat16
VMEM = pl.BlockSpec(memory_space=pltpu.VMEM)
SMEM = pl.BlockSpec(memory_space=pltpu.SMEM)
ANY = pl.BlockSpec(memory_space=pl.ANY)
HBM = pl.BlockSpec(memory_space=pltpu.HBM)


def shape(dims, dtype):
    return jax.ShapeDtypeStruct(dims, dtype)


def params(mib):
    return pltpu.CompilerParams(vmem_limit_bytes=mib << 20)


def turn(x, c, s):
    return x * c + pltpu.roll(x, HD // 2, 1) * s


def unturn(x, c, s):
    return x * c - pltpu.roll(x, HD // 2, 1) * s


def dot_t(a, b):
    return lax.dot_general(a, b, (((1,), (1,)), ((), ())), preferred_element_type=f32)


def two_parts(x):
    high = lax.reduce_precision(x, 8, 7)
    return jnp.concatenate([high, x - high], axis=-1).astype(bf16)


def angle_tables():
    half = HD // 2
    freq = rope_base ** (-(jnp.arange(half, dtype=f32) * 2.0) / HD)
    freq = jnp.concatenate([freq, freq])[None]
    steps = jnp.arange(BLK, dtype=f32)[:, None]
    out = []
    for angle in (steps * BLK * freq, steps * freq):
        out.append(two_parts(jnp.concatenate([jnp.cos(angle), jnp.sin(angle)], axis=-1)))
    return jnp.stack(out)


def full_table(pos):
    half = HD // 2
    freq = rope_base ** (-(jnp.arange(half, dtype=f32) * 2.0) / HD)
    angle = pos.astype(f32)[:, None] * freq
    cosine, sine = jnp.cos(angle), jnp.sin(angle)
    return jnp.concatenate([cosine, cosine, -sine, sine], axis=-1)


def pack_kv_kernel(k_hbm, v_hbm, pos_hbm, kv_ref, k_ref, v_ref, pos_ref, sems):
    copies = [
        pltpu.make_async_copy(src, dst, sems.at[i])
        for i, (src, dst) in enumerate(((k_hbm, k_ref), (v_hbm, v_ref), (pos_hbm, pos_ref)))
    ]
    for copy in copies:
        copy.start()
    for copy in copies:
        copy.wait()
    pos = pos_ref[...]
    high = jnp.broadcast_to((pos >> 7).astype(f32), (EXTRA, BLK)).astype(bf16)
    low = jnp.broadcast_to((pos & 127).astype(f32), (EXTRA, BLK)).astype(bf16)
    n = kv_ref.shape[0]
    for i in range(n):
        head = (i // (n // 2)) * 2 + i % 2
        cols = slice(head * HD, (head + 1) * HD)
        kv_ref[i, :BLK, :HD] = k_ref[:, cols]
        kv_ref[i, :BLK, HD:] = v_ref[:, cols]
        kv_ref[i, BLK:, :HD] = high
        kv_ref[i, BLK:, HD:] = low


def pack_kv(keys, values, positions, n):
    return pl.pallas_call(
        pack_kv_kernel,
        out_shape=shape((n, BLK + EXTRA, 2 * HD), bf16),
        in_specs=[HBM] * 3,
        out_specs=VMEM,
        scratch_shapes=[
            pltpu.VMEM(keys.shape, bf16),
            pltpu.VMEM(values.shape, bf16),
            pltpu.VMEM(positions.shape, jnp.int32),
            pltpu.SemaphoreType.DMA((3,)),
        ],
        compiler_params=params(60),
        cost_estimate=pl.CostEstimate(flops=0, bytes_accessed=2 << 20, transcendentals=0),
        name="pack_kv",
    )(keys, values, positions)


def pack_kernel(place_ref, q_ref, d_ref, own_ref, x_ref, za_ref, da_ref, zb_ref, db_ref, sems):
    mine = place_ref[0]
    targets = [
        (x_ref.at[0], 2, 0), (x_ref.at[1], 2, 1), (za_ref, 1, 0), (da_ref, 3, 0), (zb_ref, 1, 1), (db_ref, 3, 1),
        (own_ref.at[0], 0, 0), (own_ref.at[1], 0, 1),
    ]
    copies = []
    for out, flip, sub in targets:
        for which, ref in enumerate((q_ref, d_ref)):
            for h in range(SUB):
                at = pl.multiple_of((((mine ^ flip) * 2 + sub) * SUB + h) * HD, HD)
                copies.append(
                    pltpu.make_async_copy(ref.at[:, pl.ds(at, HD)], out.at[which, h], sems.at[len(copies)])
                )
                copies[-1].start()
    for copy in copies:
        copy.wait()


def pack(place, query, grad_out):
    one = shape((2, SUB, BLK, HD), bf16)
    both = shape((2, 2, SUB, BLK, HD), bf16)
    return pl.pallas_call(
        pack_kernel,
        out_shape=(both, both, one, one, one, one),
        in_specs=[SMEM] + [HBM] * 2,
        out_specs=(HBM,) * 6,
        scratch_shapes=[pltpu.SemaphoreType.DMA((2 * HQ,))],
        compiler_params=params(4),
        cost_estimate=pl.CostEstimate(flops=0, bytes_accessed=4 << 20, transcendentals=0),
        name="pack",
    )(place, query, grad_out)


def prep_kernel(kv_ref, table_ref, ks_ref, cs_ref, kr_ref, kt_ref):
    n = kv_ref.shape[0]
    sign = jnp.where(lax.broadcasted_iota(jnp.int32, (BLK, HD), 1) < HD // 2, -1.0, 1.0)
    row = lax.broadcasted_iota(jnp.int32, (BLK, BLK), 0).astype(f32)

    def pick(i, part):
        pos = kv_ref[i, BLK : BLK + EXTRA, part * HD : (part + 1) * HD].astype(f32)[:1]
        hot = jnp.where(row == pos, 1.0, 0.0).T.astype(bf16)
        got = jnp.dot(hot, table_ref[part], preferred_element_type=f32)
        got = got[:, : 2 * HD] + got[:, 2 * HD :]
        return got[:, :HD], got[:, HD:]

    per = KEYS // BLK

    def ready(w, carry):
        for j in range(per):
            i = w * per + j
            at = pl.ds(pl.multiple_of(i * BLK, BLK), BLK)
            ch, sh = pick(i, 0)
            cl, sl = pick(i, 1)
            c = ch * cl - sh * sl
            s = (sh * cl + ch * sl) * sign
            cs_ref[at, :HD] = c
            cs_ref[at, HD:] = s
            r = turn(kv_ref[i, :BLK, :HD].astype(f32) * ks_ref[...], c, s)
            kr_ref[at, :] = r.astype(bf16)
            kt_ref[w, :, j * BLK : (j + 1) * BLK] = r.T.astype(bf16)
        return carry

    lax.fori_loop(0, n // per, ready, 0)


def prep(kv, table, ks):
    length = kv.shape[0] * BLK
    return pl.pallas_call(
        prep_kernel,
        out_shape=(
            shape((length, 2 * HD), f32),
            shape((length, HD), bf16),
            shape((length // KEYS, HD, KEYS), bf16),
        ),
        in_specs=[VMEM] * 3,
        out_specs=(VMEM,) * 3,
        compiler_params=params(12),
        cost_estimate=pl.CostEstimate(flops=1 << 29, bytes_accessed=5 << 20, transcendentals=0),
        name="prep",
    )(kv, table, ks)


def attend_kernel(stage, blocks_ref, *refs):
    take = iter(refs)
    get = lambda count: [next(take) for _ in range(count)]
    parts = get(2 if stage == 0 else 4)
    kv_hbm, cs_hbm, kr_hbm, kt_hbm, qs_ref = get(5)
    dk_in, dv_in, tq_in = get(3) if stage else (None,) * 3
    grads = get(2 if stage == 0 else 4)
    last = get(3 if stage == 0 else 2)
    s_scr, p_scr, qd_scr, kv_ref, cs_ref, kr_ref, kt_ref, q_scr, dq_scr, m_scr, e_scr, gq_scr, dk_ref, dv_ref = get(14)
    tq_ref, sems, kv_sems = get(3)
    n = kv_ref.shape[0]
    first, second = pl.ds(0, SUB), pl.ds(SUB, SUB)
    if stage == 0:
        places = lambda r: ((r[0].at[0], 0, first), (r[0].at[1], 0, second), (r[1].at[0], 1, first), (r[1].at[1], 1, second))
    else:
        places = lambda r: ((r[0], 0, first), (r[2], 0, second), (r[1], 1, first), (r[3], 1, second))
    pieces = [(src, qd_scr.at[u, :, heads]) for src, u, heads in places(parts)]
    pieces += [(kr_hbm, kr_ref), (kv_hbm, kv_ref), (cs_hbm, cs_ref), (kt_hbm, kt_ref)]
    if stage:
        pieces += [(dk_in, dk_ref), (dv_in, dv_ref)]
    copies = [pltpu.make_async_copy(src, dst, kv_sems.at[i]) for i, (src, dst) in enumerate(pieces)]
    for copy in copies:
        copy.start()
    if stage == 0:
        dk_ref[...] = jnp.zeros_like(dk_ref)
        dv_ref[...] = jnp.zeros_like(dv_ref)
        tq_ref[...] = jnp.zeros_like(tq_ref)
    else:
        tq_ref[...] = tq_in[...]
    rows, (kr_copy, kv_copy, cs_copy, kt_copy), sums = copies[:4], copies[4:8], copies[8:]
    per = KEYS // BLK

    def wait(u, *which):
        @pl.when(u == 0)
        def _():
            for copy in which:
                copy.wait()

    sub8 = lax.broadcasted_iota(jnp.int32, (8, ROWS), 0)
    lane = lax.broadcasted_iota(jnp.int32, (8, ROWS), 1)
    group = lax.broadcasted_iota(jnp.int32, (CHUNK // 8, 8, ROWS), 0) * 8

    def unit(u, carry):
        b0, b1 = blocks_ref[2 * u], blocks_ref[2 * u + 1]
        wait(u, *rows, cs_copy)
        tabs = []
        for b in (b0, b1):
            toks = pl.ds(pl.multiple_of(b * BLK, BLK), BLK)
            tabs.append((cs_ref[toks, :HD], cs_ref[toks, HD:]))
        for h in range(2 * SUB):
            cols = slice(h * BLK, (h + 1) * BLK)
            r = turn(qd_scr[u, 0, h].astype(f32) * qs_ref[h : h + 1, :], *tabs[h // SUB])
            q_scr[cols, :] = r.astype(bf16)
        dq_scr[...] = jnp.zeros_like(dq_scr)
        token = jnp.where(lane < ROWS // 2, b0, b1) * BLK + (lane & (BLK - 1)) - sub8
        steps = jnp.maximum(b0, b1) // per + 1

        wait(u, kr_copy, kv_copy)

        def look(w, stats, masked):
            m, l, d = stats
            for j in range(KEYS // CHUNK):
                at = pl.ds(pl.multiple_of(w * KEYS + j * CHUNK, CHUNK), CHUNK)
                vals = kv_ref[pl.ds(w * per + j * (CHUNK // BLK), CHUNK // BLK), :BLK, HD:]
                s = dot_t(kr_ref[at, :], q_scr[...]) * EXP2
                dp = dot_t(vals.reshape(CHUNK, HD), qd_scr[u, 1].reshape(ROWS, HD))
                p_scr[at, :] = dp
                s3 = s.reshape(CHUNK // 8, 8, ROWS)
                dp3 = dp.reshape(CHUNK // 8, 8, ROWS)
                if masked:
                    s3 = jnp.where(group <= (token - (w * KEYS + j * CHUNK))[None], s3, NEG)
                s_scr[at, :] = s3.reshape(CHUNK, ROWS)
                mn = jnp.maximum(m, jnp.max(s3, axis=0))
                a = jnp.exp2(m - mn)
                e = jnp.exp2(s3 - mn[None])
                m, l, d = mn, l * a + jnp.sum(e, axis=0), d * a + jnp.sum(e * dp3, axis=0)
            return m, l, d

        zero = jnp.zeros((8, ROWS), f32)
        stats = (zero + NEG, zero, zero)
        clear = jnp.minimum(b0, b1) // per
        stats = lax.fori_loop(0, clear, lambda w, c: look(w, c, False), stats)
        m, l, d = lax.fori_loop(clear, steps, lambda w, c: look(w, c, True), stats)
        top = jnp.max(m, axis=0, keepdims=True)
        w = jnp.exp2(m - top)
        total = jnp.sum(l * w, axis=0, keepdims=True)
        delta = jnp.sum(d * w, axis=0, keepdims=True) / total
        shift = top + jnp.log2(total)
        m_scr[...] = jnp.broadcast_to(shift, m_scr.shape)
        e_scr[...] = jnp.broadcast_to(delta, e_scr.shape)

        wait(u, kt_copy, *sums)

        def back(w, carry):
            shift, delta = m_scr[...][None], e_scr[...][None]
            dq = dq_scr[...]
            for j in range(KEYS // CHUNK):
                at = pl.ds(pl.multiple_of(w * KEYS + j * CHUNK, CHUNK), CHUNK)
                s3 = s_scr[at, :].reshape(CHUNK // 8, 8, ROWS)
                dp3 = p_scr[at, :].reshape(CHUNK // 8, 8, ROWS)
                p = jnp.exp2(s3 - shift)
                ds = (p * (dp3 - delta)).reshape(CHUNK, ROWS).astype(bf16)
                p = p.reshape(CHUNK, ROWS).astype(bf16)
                dv_ref[at, :] += jnp.dot(p, qd_scr[u, 1].reshape(ROWS, HD), preferred_element_type=f32)
                dk_ref[at, :] += jnp.dot(ds, q_scr[...], preferred_element_type=f32)
                dq = dq + jnp.dot(
                    kt_ref[w, :, j * CHUNK : (j + 1) * CHUNK], ds, preferred_element_type=f32
                )
            dq_scr[...] = dq
            return carry

        lax.fori_loop(0, steps, back, 0)

        for h in range(2 * SUB):
            cos, sin = tabs[h // SUB]
            g = (dq_scr[:, h * BLK : (h + 1) * BLK] * FACTOR).T.astype(bf16).astype(f32)
            g = unturn(g, cos, sin)
            gq_scr[u, h] = (g * qs_ref[h : h + 1, :]).astype(bf16)
            tq_ref[h : h + 1, :] += jnp.sum(g * qd_scr[u, 0, h].astype(f32), axis=0, keepdims=True)
        return carry

    lax.fori_loop(0, 2, unit, 0)
    outs = [(gq_scr.at[u, heads], dst) for dst, u, heads in places(grads)]
    if stage == 0:
        outs += [(dk_ref, last[0]), (dv_ref, last[1])]
    copies = [pltpu.make_async_copy(src, dst, sems.at[i]) for i, (src, dst) in enumerate(outs)]
    for copy in copies:
        copy.start()
    if stage == 0:
        last[2][...] = tq_ref[...]
        for copy in copies:
            copy.wait()
        return
    term_ref, dkv_ref = last

    def finish(c, tk):
        at = pl.ds(pl.multiple_of(c * BLK, BLK), BLK)
        g = dk_ref[at, :] * FACTOR
        dkv_ref[c, :BLK, :HD] = g.astype(bf16)
        dkv_ref[c, :BLK, HD:] = dv_ref[at, :].astype(bf16)
        dkv_ref[c, BLK:, :] = jnp.zeros((EXTRA, 2 * HD), bf16)
        g = unturn(g, cs_ref[at, :HD], cs_ref[at, HD:])
        return tk + jnp.sum(g * kv_ref[c, :BLK, :HD].astype(f32), axis=0, keepdims=True)

    tk = lax.fori_loop(0, n, finish, jnp.zeros((1, HD), f32), unroll=4)
    terms = jnp.concatenate([tq_ref[...], jnp.broadcast_to(tk, (8, HD))], axis=0)
    for j in range(term_ref.shape[0]):
        term_ref[j] = terms
    for copy in copies:
        copy.wait()


def attend(stage, blocks, parts, kv, cs, kr, kt, qs, before, sequences):
    n = kv.shape[0]
    length = n * BLK
    one, both = shape((SUB, BLK, HD), bf16), shape((2, SUB, BLK, HD), bf16)
    total = shape((length, HD), f32)
    pairs = 2 * ROWS * length // 2
    if stage == 0:
        out_shape = (both, both, total, total, shape((2 * SUB, HD), f32))
        out_specs = (HBM,) * 2 + (ANY,) * 2 + (VMEM,)
    else:
        out_shape = (one,) * 4 + (shape((sequences, 2 * SUB + 8, HD), f32), shape(kv.shape, bf16))
        out_specs = (HBM,) * 4 + (VMEM,) * 2
    return pl.pallas_call(
        lambda *refs: attend_kernel(stage, *refs),
        out_shape=out_shape,
        in_specs=[SMEM] + [ANY] * (len(parts) + 4) + [VMEM] + ([ANY, ANY, VMEM] if stage else []),
        out_specs=out_specs,
        scratch_shapes=[
            pltpu.VMEM((length, ROWS), f32),
            pltpu.VMEM((length, ROWS), f32),
            pltpu.VMEM((2, 2, 2 * SUB, BLK, HD), bf16),
            pltpu.VMEM(kv.shape, bf16),
            pltpu.VMEM((length, 2 * HD), f32),
            pltpu.VMEM((length, HD), bf16),
            pltpu.VMEM((length // KEYS, HD, KEYS), bf16),
            pltpu.VMEM((ROWS, HD), bf16),
            pltpu.VMEM((HD, ROWS), f32),
            pltpu.VMEM((8, ROWS), f32),
            pltpu.VMEM((8, ROWS), f32),
            pltpu.VMEM((2, 2 * SUB, BLK, HD), bf16),
            pltpu.VMEM((length, HD), f32),
            pltpu.VMEM((length, HD), f32),
            pltpu.VMEM((2 * SUB, HD), f32),
            pltpu.SemaphoreType.DMA((6,)),
            pltpu.SemaphoreType.DMA((10,)),
        ],
        compiler_params=params(36),
        cost_estimate=pl.CostEstimate(flops=pairs * HD * 20, bytes_accessed=8 << 20, transcendentals=pairs * 2),
        name="attend",
    )(blocks, *parts, kv, cs, kr, kt, qs, *before)


def add_kernel(term_ref, dkv_in, dkv_ref, pair, sems):
    total = jnp.sum(term_ref[...], axis=0)
    high = total.astype(bf16)
    pair[:, :HD] = high
    pair[:, HD:] = (total - high.astype(f32)).astype(bf16)
    copies = [
        pltpu.make_async_copy(pair, dkv_ref.at[i, pl.ds(BLK, EXTRA)], sems.at[i])
        for i in range(dkv_ref.shape[0])
    ]
    for copy in copies:
        copy.start()
    for copy in copies:
        copy.wait()


def add(term, dkv):
    return pl.pallas_call(
        add_kernel,
        out_shape=shape(dkv.shape, bf16),
        in_specs=[VMEM, ANY],
        out_specs=ANY,
        scratch_shapes=[pltpu.VMEM((EXTRA, 2 * HD), bf16), pltpu.SemaphoreType.DMA((dkv.shape[0],))],
        input_output_aliases={1: 0},
        compiler_params=params(8),
        name="add",
    )(term, dkv)


def unpack_kernel(place_ref, own_ref, x_ref, za_ref, da_ref, zb_ref, db_ref, out_ref):
    mine = place_ref[0]

    def put(src, head, sub):
        for h in range(SUB):
            at = pl.multiple_of(((head * 2 + sub) * SUB + h) * HD, HD)
            out_ref[:, pl.ds(at, HD)] = src[h]

    for sub in range(2):
        put(own_ref.at[sub], mine, sub)
        put(x_ref.at[sub], mine ^ 2, sub)
    put(za_ref, mine ^ 1, 0)
    put(da_ref, mine ^ 3, 0)
    put(zb_ref, mine ^ 1, 1)
    put(db_ref, mine ^ 3, 1)


def unpack(place, parts):
    return pl.pallas_call(
        unpack_kernel,
        out_shape=shape((BLK, HQ * HD), bf16),
        in_specs=[SMEM] + [VMEM] * 6,
        out_specs=VMEM,
        compiler_params=params(8),
        cost_estimate=pl.CostEstimate(flops=0, bytes_accessed=2 << 20, transcendentals=0),
        name="unpack",
    )(place, *parts)


def final_kernel(dkv_ref, tab, ks_ref, gk_ref, gv_ref, tq_ref, tk_ref):
    n = dkv_ref.shape[0]
    for head in range(HK):
        first = (head // 2) * (n // 2) + head % 2
        got = jnp.zeros((BLK + EXTRA, 2 * HD), f32)
        for i in range(first, first + n // 2, 2):
            got = got + dkv_ref[i].astype(f32)
        cols = slice(head * HD, (head + 1) * HD)
        g = unturn(got[:BLK, :HD].astype(bf16).astype(f32), tab[:, :HD], tab[:, HD:])
        gk_ref[:, cols] = (g * ks_ref[head : head + 1, :]).astype(bf16)
        gv_ref[:, cols] = got[:BLK, HD:].astype(bf16)
        term = got[BLK:, :HD] + got[BLK:, HD:]
        tq_ref[head * 2 * SUB : (head + 1) * 2 * SUB, :] = term[: 2 * SUB]
        tk_ref[head : head + 1, :] = term[2 * SUB : 2 * SUB + 1]


def final(dkv, table, ks):
    return pl.pallas_call(
        final_kernel,
        out_shape=(
            shape((BLK, HK * HD), bf16),
            shape((BLK, HK * HD), bf16),
            shape((HQ, HD), f32),
            shape((HK, HD), f32),
        ),
        in_specs=[VMEM] * 3,
        out_specs=(VMEM,) * 4,
        compiler_params=params(8),
        name="final",
    )(dkv, table, ks)


def shards(query, keys, values, grad_out, positions, q_scale, k_scale):
    n = lax.axis_size("seq")
    half = n // 2
    me = lax.axis_index("seq")
    x, z = me // half, me % half
    odd = z % 2
    kind = x * 2 + odd
    place = jnp.stack([kind, me]).astype(jnp.int32)
    za = z + 1 - 2 * odd
    zb = (z - 1 + 2 * odd) % half

    def pairs(flip, step):
        out = []
        for i in range(n):
            xi, zi = i // half, i % half
            zo = (zi + step * (1 - 2 * (zi % 2))) % half
            out.append((i, (xi ^ flip) * half + zo))
        return out

    def send(a, flip, step):
        return lax.ppermute(a, "seq", pairs(flip, step))

    kv = lax.all_to_all(pack_kv(keys[0], values[0], positions, n), "seq", 0, 0, tiled=True)
    own, to_x, to_za, to_da, to_zb, to_db = pack(place, query[0], grad_out[0])
    in_x = send(to_x, 1, 0)
    in_za, in_da = send(to_za, 0, 1), send(to_da, 1, 1)
    in_zb, in_db = send(to_zb, 0, -1), send(to_db, 1, -1)

    q_gain = lax.dynamic_slice_in_dim(q_scale.reshape(HK, 2 * SUB, HD), kind, 1, 0)[0]
    k_gain = lax.dynamic_slice_in_dim(k_scale.reshape(HK, HD), kind, 1, 0)
    keys_side = (kv, *prep(kv, angle_tables(), k_gain))
    sequences = lax.axis_size("dp")
    blocks = jnp.stack([me, me, me ^ half, me ^ half]).astype(jnp.int32)
    go, gx, *sums = attend(0, blocks, (own, in_x), *keys_side, q_gain, (), sequences)
    pair = lambda side: [side * half + za, side * half + zb]
    blocks = jnp.stack(pair(x) + pair(1 - x)).astype(jnp.int32)
    gza, gda, gzb, gdb, term, dkv = attend(
        1, blocks, (in_za, in_da, in_zb, in_db), *keys_side, q_gain, sums, sequences
    )

    term = lax.all_to_all(term, "dp", 0, 0, tiled=True)
    back = (go, send(gx, 1, 0), send(gza, 0, 1), send(gda, 1, 1), send(gzb, 0, -1), send(gdb, 1, -1))
    dkv, back = lax.optimization_barrier((add(term, dkv), back))
    dkv = lax.all_to_all(dkv, "seq", 0, 0, tiled=True)
    grad_query = unpack(place, back)
    grad_keys, grad_values, total_q, total_k = final(
        dkv, full_table(positions[0]), k_scale.reshape(HK, HD)
    )
    return (
        grad_query[None],
        grad_keys[None],
        grad_values[None],
        total_q.reshape(HQ * HD),
        total_k.reshape(HK * HD),
    )


def solution(mesh):
    return jax.shard_map(
        shards,
        mesh=mesh,
        in_specs=(
            P("dp", "seq", None),
            P("dp", "seq", None),
            P("dp", "seq", None),
            P("dp", "seq", None),
            P("dp", "seq"),
            P(),
            P(),
        ),
        out_specs=(P("dp", "seq", None), P("dp", "seq", None), P("dp", "seq", None), P(), P()),
        check_vma=False,
    )
```

```python
import math

import jax
import jax.numpy as jnp
from jax import lax
from jax.experimental import pallas as pl
from jax.experimental.pallas import tpu as pltpu
from jax.sharding import PartitionSpec as P

HQ = 32
HK = 4
HD = 128
BLK = 128
EXTRA = 16
SUB = 4
ROWS = 2 * SUB * BLK
CHUNK = 256
KEYS = 512
FACTOR = 1.0 / math.sqrt(HD)
EXP2 = FACTOR * math.log2(math.e)
NEG = -1e30
rope_base = 1000000.0

f32 = jnp.float32
bf16 = jnp.bfloat16
VMEM = pl.BlockSpec(memory_space=pltpu.VMEM)
SMEM = pl.BlockSpec(memory_space=pltpu.SMEM)
ANY = pl.BlockSpec(memory_space=pl.ANY)
HBM = pl.BlockSpec(memory_space=pltpu.HBM)


def shape(dims, dtype):
    return jax.ShapeDtypeStruct(dims, dtype)


def params(mib):
    return pltpu.CompilerParams(vmem_limit_bytes=mib << 20)


def turn(x, c, s):
    return x * c + pltpu.roll(x, HD // 2, 1) * s


def unturn(x, c, s):
    return x * c - pltpu.roll(x, HD // 2, 1) * s


def dot_t(a, b):
    return lax.dot_general(a, b, (((1,), (1,)), ((), ())), preferred_element_type=f32)


def two_parts(x):
    high = lax.reduce_precision(x, 8, 7)
    return jnp.concatenate([high, x - high], axis=-1).astype(bf16)


def angle_tables():
    half = HD // 2
    freq = rope_base ** (-(jnp.arange(half, dtype=f32) * 2.0) / HD)
    freq = jnp.concatenate([freq, freq])[None]
    steps = jnp.arange(BLK, dtype=f32)[:, None]
    out = []
    for angle in (steps * BLK * freq, steps * freq):
        out.append(two_parts(jnp.concatenate([jnp.cos(angle), jnp.sin(angle)], axis=-1)))
    return jnp.stack(out)


def full_table(pos):
    half = HD // 2
    freq = rope_base ** (-(jnp.arange(half, dtype=f32) * 2.0) / HD)
    angle = pos.astype(f32)[:, None] * freq
    cosine, sine = jnp.cos(angle), jnp.sin(angle)
    return jnp.concatenate([cosine, cosine, -sine, sine], axis=-1)


def pack_kv_kernel(k_hbm, v_hbm, pos_hbm, kv_ref, k_ref, v_ref, pos_ref, sems):
    copies = [
        pltpu.make_async_copy(src, dst, sems.at[i])
        for i, (src, dst) in enumerate(((k_hbm, k_ref), (v_hbm, v_ref), (pos_hbm, pos_ref)))
    ]
    for copy in copies:
        copy.start()
    for copy in copies:
        copy.wait()
    pos = pos_ref[...]
    high = jnp.broadcast_to((pos >> 7).astype(f32), (EXTRA, BLK)).astype(bf16)
    low = jnp.broadcast_to((pos & 127).astype(f32), (EXTRA, BLK)).astype(bf16)
    n = kv_ref.shape[0]
    for i in range(n):
        head = (i // (n // 2)) * 2 + i % 2
        cols = slice(head * HD, (head + 1) * HD)
        kv_ref[i, :BLK, :HD] = k_ref[:, cols]
        kv_ref[i, :BLK, HD:] = v_ref[:, cols]
        kv_ref[i, BLK:, :HD] = high
        kv_ref[i, BLK:, HD:] = low


def pack_kv(keys, values, positions, n):
    return pl.pallas_call(
        pack_kv_kernel,
        out_shape=shape((n, BLK + EXTRA, 2 * HD), bf16),
        in_specs=[HBM] * 3,
        out_specs=VMEM,
        scratch_shapes=[
            pltpu.VMEM(keys.shape, bf16),
            pltpu.VMEM(values.shape, bf16),
            pltpu.VMEM(positions.shape, jnp.int32),
            pltpu.SemaphoreType.DMA((3,)),
        ],
        compiler_params=params(60),
        cost_estimate=pl.CostEstimate(flops=0, bytes_accessed=2 << 20, transcendentals=0),
        name="pack_kv",
    )(keys, values, positions)


def pack_kernel(place_ref, q_ref, d_ref, own_ref, x_ref, za_ref, da_ref, zb_ref, db_ref, sems):
    mine = place_ref[0]
    targets = [
        (x_ref.at[0], 2, 0), (x_ref.at[1], 2, 1), (za_ref, 1, 0), (da_ref, 3, 0), (zb_ref, 1, 1), (db_ref, 3, 1),
        (own_ref.at[0], 0, 0), (own_ref.at[1], 0, 1),
    ]
    copies = []
    for out, flip, sub in targets:
        for which, ref in enumerate((q_ref, d_ref)):
            for h in range(SUB):
                at = pl.multiple_of((((mine ^ flip) * 2 + sub) * SUB + h) * HD, HD)
                copies.append(
                    pltpu.make_async_copy(ref.at[:, pl.ds(at, HD)], out.at[which, h], sems.at[len(copies)])
                )
                copies[-1].start()
    for copy in copies:
        copy.wait()


def pack(place, query, grad_out):
    one = shape((2, SUB, BLK, HD), bf16)
    both = shape((2, 2, SUB, BLK, HD), bf16)
    return pl.pallas_call(
        pack_kernel,
        out_shape=(both, both, one, one, one, one),
        in_specs=[SMEM] + [HBM] * 2,
        out_specs=(HBM,) * 6,
        scratch_shapes=[pltpu.SemaphoreType.DMA((2 * HQ,))],
        compiler_params=params(4),
        cost_estimate=pl.CostEstimate(flops=0, bytes_accessed=4 << 20, transcendentals=0),
        name="pack",
    )(place, query, grad_out)


def prep_kernel(kv_ref, table_ref, ks_ref, cs_ref, kr_ref, kt_ref):
    n = kv_ref.shape[0]
    sign = jnp.where(lax.broadcasted_iota(jnp.int32, (BLK, HD), 1) < HD // 2, -1.0, 1.0)
    row = lax.broadcasted_iota(jnp.int32, (BLK, BLK), 0).astype(f32)

    def pick(i, part):
        pos = kv_ref[i, BLK : BLK + EXTRA, part * HD : (part + 1) * HD].astype(f32)[:1]
        hot = jnp.where(row == pos, 1.0, 0.0).T.astype(bf16)
        got = jnp.dot(hot, table_ref[part], preferred_element_type=f32)
        got = got[:, : 2 * HD] + got[:, 2 * HD :]
        return got[:, :HD], got[:, HD:]

    per = KEYS // BLK

    def ready(w, carry):
        for j in range(per):
            i = w * per + j
            at = pl.ds(pl.multiple_of(i * BLK, BLK), BLK)
            ch, sh = pick(i, 0)
            cl, sl = pick(i, 1)
            c = ch * cl - sh * sl
            s = (sh * cl + ch * sl) * sign
            cs_ref[at, :HD] = c
            cs_ref[at, HD:] = s
            r = turn(kv_ref[i, :BLK, :HD].astype(f32) * ks_ref[...], c, s)
            kr_ref[at, :] = r.astype(bf16)
            kt_ref[w, :, j * BLK : (j + 1) * BLK] = r.T.astype(bf16)
        return carry

    lax.fori_loop(0, n // per, ready, 0, unroll=2)


def prep(kv, table, ks):
    length = kv.shape[0] * BLK
    return pl.pallas_call(
        prep_kernel,
        out_shape=(
            shape((length, 2 * HD), f32),
            shape((length, HD), bf16),
            shape((length // KEYS, HD, KEYS), bf16),
        ),
        in_specs=[VMEM] * 3,
        out_specs=(VMEM,) * 3,
        compiler_params=params(12),
        cost_estimate=pl.CostEstimate(flops=1 << 29, bytes_accessed=5 << 20, transcendentals=0),
        name="prep",
    )(kv, table, ks)


def attend_kernel(stage, blocks_ref, *refs):
    take = iter(refs)
    get = lambda count: [next(take) for _ in range(count)]
    parts = get(2 if stage == 0 else 4)
    kv_ref, cs_ref, kr_ref, kt_ref, qs_ref = get(5)
    dk_in, dv_in, tq_in = get(3) if stage else (None,) * 3
    grads = get(2 if stage == 0 else 4)
    last = get(3 if stage == 0 else 2)
    s_scr, p_scr, qd_scr, q_scr, dq_scr, m_scr, e_scr, gq_scr, dk_ref, dv_ref = get(10)
    tq_ref, sems, kv_sems = get(3)
    n = kv_ref.shape[0]
    first, second = pl.ds(0, SUB), pl.ds(SUB, SUB)
    if stage == 0:
        places = lambda r: ((r[0].at[0], 0, first), (r[0].at[1], 0, second), (r[1].at[0], 1, first), (r[1].at[1], 1, second))
    else:
        places = lambda r: ((r[0], 0, first), (r[2], 0, second), (r[1], 1, first), (r[3], 1, second))
    pieces = [(src, qd_scr.at[u, :, heads]) for src, u, heads in places(parts)]
    if stage:
        pieces += [(dk_in, dk_ref), (dv_in, dv_ref)]
    copies = [pltpu.make_async_copy(src, dst, kv_sems.at[i]) for i, (src, dst) in enumerate(pieces)]
    for copy in copies:
        copy.start()
    if stage == 0:
        dk_ref[...] = jnp.zeros_like(dk_ref)
        dv_ref[...] = jnp.zeros_like(dv_ref)
        tq_ref[...] = jnp.zeros_like(tq_ref)
    else:
        tq_ref[...] = tq_in[...]
    rows, sums = copies[:4], copies[4:]
    per = KEYS // BLK

    outs = [(gq_scr.at[u, heads], dst) for dst, u, heads in places(grads)]
    if stage == 0:
        outs += [(dk_ref, last[0]), (dv_ref, last[1])]
    copies = [pltpu.make_async_copy(src, dst, sems.at[i]) for i, (src, dst) in enumerate(outs)]

    def wait(u, at, *which):
        @pl.when(u == at)
        def _():
            for copy in which:
                copy.wait()

    sub8 = lax.broadcasted_iota(jnp.int32, (8, ROWS), 0)
    lane = lax.broadcasted_iota(jnp.int32, (8, ROWS), 1)
    group = lax.broadcasted_iota(jnp.int32, (CHUNK // 8, 8, ROWS), 0) * 8

    def unit(u, carry):
        b0, b1 = blocks_ref[2 * u], blocks_ref[2 * u + 1]
        wait(u, 0, *rows[:2])
        wait(u, 1, *rows[2:])
        tabs = []
        for b in (b0, b1):
            toks = pl.ds(pl.multiple_of(b * BLK, BLK), BLK)
            tabs.append((cs_ref[toks, :HD], cs_ref[toks, HD:]))
        for h in range(2 * SUB):
            cols = slice(h * BLK, (h + 1) * BLK)
            r = turn(qd_scr[u, 0, h].astype(f32) * qs_ref[h : h + 1, :], *tabs[h // SUB])
            q_scr[cols, :] = r.astype(bf16)
        dq_scr[...] = jnp.zeros_like(dq_scr)
        token = jnp.where(lane < ROWS // 2, b0, b1) * BLK + (lane & (BLK - 1)) - sub8
        steps = jnp.maximum(b0, b1) // per + 1

        def look(w, stats, masked):
            m, l, d = stats
            for j in range(KEYS // CHUNK):
                at = pl.ds(pl.multiple_of(w * KEYS + j * CHUNK, CHUNK), CHUNK)
                vals = kv_ref[pl.ds(w * per + j * (CHUNK // BLK), CHUNK // BLK), :BLK, HD:]
                s = dot_t(kr_ref[at, :], q_scr[...]) * EXP2
                dp = dot_t(vals.reshape(CHUNK, HD), qd_scr[u, 1].reshape(ROWS, HD))
                p_scr[at, :] = dp
                s3 = s.reshape(CHUNK // 8, 8, ROWS)
                dp3 = dp.reshape(CHUNK // 8, 8, ROWS)
                if masked:
                    s3 = jnp.where(group <= (token - (w * KEYS + j * CHUNK))[None], s3, NEG)
                s_scr[at, :] = s3.reshape(CHUNK, ROWS)
                mn = jnp.maximum(m, jnp.max(s3, axis=0))
                a = jnp.exp2(m - mn)
                e = jnp.exp2(s3 - mn[None])
                m, l, d = mn, l * a + jnp.sum(e, axis=0), d * a + jnp.sum(e * dp3, axis=0)
            return m, l, d

        zero = jnp.zeros((8, ROWS), f32)
        stats = (zero + NEG, zero, zero)
        clear = jnp.minimum(b0, b1) // per
        stats = lax.fori_loop(0, clear, lambda w, c: look(w, c, False), stats)
        m, l, d = lax.fori_loop(clear, steps, lambda w, c: look(w, c, True), stats)
        top = jnp.max(m, axis=0, keepdims=True)
        w = jnp.exp2(m - top)
        total = jnp.sum(l * w, axis=0, keepdims=True)
        delta = jnp.sum(d * w, axis=0, keepdims=True) / total
        shift = top + jnp.log2(total)
        m_scr[...] = jnp.broadcast_to(shift, m_scr.shape)
        e_scr[...] = jnp.broadcast_to(delta, e_scr.shape)

        wait(u, 0, *sums)

        def back(w, carry):
            shift, delta = m_scr[...][None], e_scr[...][None]
            dq = dq_scr[...]
            for j in range(KEYS // CHUNK):
                at = pl.ds(pl.multiple_of(w * KEYS + j * CHUNK, CHUNK), CHUNK)
                s3 = s_scr[at, :].reshape(CHUNK // 8, 8, ROWS)
                dp3 = p_scr[at, :].reshape(CHUNK // 8, 8, ROWS)
                p = jnp.exp2(s3 - shift)
                ds = (p * (dp3 - delta)).reshape(CHUNK, ROWS).astype(bf16)
                p = p.reshape(CHUNK, ROWS).astype(bf16)
                dv_ref[at, :] += jnp.dot(p, qd_scr[u, 1].reshape(ROWS, HD), preferred_element_type=f32)
                dk_ref[at, :] += jnp.dot(ds, q_scr[...], preferred_element_type=f32)
                dq = dq + jnp.dot(
                    kt_ref[w, :, j * CHUNK : (j + 1) * CHUNK], ds, preferred_element_type=f32
                )
            dq_scr[...] = dq
            return carry

        lax.fori_loop(0, steps, back, 0)

        for h in range(2 * SUB):
            cos, sin = tabs[h // SUB]
            g = (dq_scr[:, h * BLK : (h + 1) * BLK] * FACTOR).T.astype(bf16).astype(f32)
            g = unturn(g, cos, sin)
            gq_scr[u, h] = (g * qs_ref[h : h + 1, :]).astype(bf16)
            tq_ref[h : h + 1, :] += jnp.sum(g * qd_scr[u, 0, h].astype(f32), axis=0, keepdims=True)
        for i in range(2):

            @pl.when(u == i)
            def _():
                for copy in copies[2 * i : 2 * i + 2]:
                    copy.start()

        return carry

    lax.fori_loop(0, 2, unit, 0)
    if stage == 0:
        for copy in copies[4:]:
            copy.start()
    if stage == 0:
        last[2][...] = tq_ref[...]
        for copy in copies:
            copy.wait()
        return
    term_ref, dkv_ref = last

    def finish(c, tk):
        at = pl.ds(pl.multiple_of(c * BLK, BLK), BLK)
        g = dk_ref[at, :] * FACTOR
        dkv_ref[c, :BLK, :HD] = g.astype(bf16)
        dkv_ref[c, :BLK, HD:] = dv_ref[at, :].astype(bf16)
        dkv_ref[c, BLK:, :] = jnp.zeros((EXTRA, 2 * HD), bf16)
        g = unturn(g, cs_ref[at, :HD], cs_ref[at, HD:])
        return tk + jnp.sum(g * kv_ref[c, :BLK, :HD].astype(f32), axis=0, keepdims=True)

    tk = lax.fori_loop(0, n, finish, jnp.zeros((1, HD), f32), unroll=4)
    terms = jnp.concatenate([tq_ref[...], jnp.broadcast_to(tk, (8, HD))], axis=0)
    for j in range(term_ref.shape[0]):
        term_ref[j] = terms
    for copy in copies:
        copy.wait()


def attend(stage, blocks, parts, kv, cs, kr, kt, qs, before, sequences):
    n = kv.shape[0]
    length = n * BLK
    one, both = shape((SUB, BLK, HD), bf16), shape((2, SUB, BLK, HD), bf16)
    total = shape((length, HD), f32)
    pairs = 2 * ROWS * length // 2
    if stage == 0:
        out_shape = (both, both, total, total, shape((2 * SUB, HD), f32))
        out_specs = (HBM,) * 2 + (ANY,) * 2 + (VMEM,)
    else:
        out_shape = (one,) * 4 + (shape((sequences, 2 * SUB + 8, HD), f32), shape(kv.shape, bf16))
        out_specs = (HBM,) * 4 + (VMEM,) * 2
    return pl.pallas_call(
        lambda *refs: attend_kernel(stage, *refs),
        out_shape=out_shape,
        in_specs=[SMEM] + [ANY] * len(parts) + [VMEM] * 5 + ([ANY, ANY, VMEM] if stage else []),
        out_specs=out_specs,
        scratch_shapes=[
            pltpu.VMEM((length, ROWS), f32),
            pltpu.VMEM((length, ROWS), f32),
            pltpu.VMEM((2, 2, 2 * SUB, BLK, HD), bf16),
            pltpu.VMEM((ROWS, HD), bf16),
            pltpu.VMEM((HD, ROWS), f32),
            pltpu.VMEM((8, ROWS), f32),
            pltpu.VMEM((8, ROWS), f32),
            pltpu.VMEM((2, 2 * SUB, BLK, HD), bf16),
            pltpu.VMEM((length, HD), f32),
            pltpu.VMEM((length, HD), f32),
            pltpu.VMEM((2 * SUB, HD), f32),
            pltpu.SemaphoreType.DMA((6,)),
            pltpu.SemaphoreType.DMA((10,)),
        ],
        compiler_params=params(36),
        cost_estimate=pl.CostEstimate(flops=pairs * HD * 20, bytes_accessed=8 << 20, transcendentals=pairs * 2),
        name="attend",
    )(blocks, *parts, kv, cs, kr, kt, qs, *before)


def add_kernel(term_ref, dkv_in, dkv_ref, pair, sems):
    total = jnp.sum(term_ref[...], axis=0)
    high = total.astype(bf16)
    pair[:, :HD] = high
    pair[:, HD:] = (total - high.astype(f32)).astype(bf16)
    copies = [
        pltpu.make_async_copy(pair, dkv_ref.at[i, pl.ds(BLK, EXTRA)], sems.at[i])
        for i in range(dkv_ref.shape[0])
    ]
    for copy in copies:
        copy.start()
    for copy in copies:
        copy.wait()


def add(term, dkv):
    return pl.pallas_call(
        add_kernel,
        out_shape=shape(dkv.shape, bf16),
        in_specs=[VMEM, ANY],
        out_specs=ANY,
        scratch_shapes=[pltpu.VMEM((EXTRA, 2 * HD), bf16), pltpu.SemaphoreType.DMA((dkv.shape[0],))],
        input_output_aliases={1: 0},
        compiler_params=params(8),
        name="add",
    )(term, dkv)


def unpack_kernel(place_ref, own_ref, x_ref, za_ref, da_ref, zb_ref, db_ref, out_ref):
    mine = place_ref[0]

    def put(src, head, sub):
        for h in range(SUB):
            at = pl.multiple_of(((head * 2 + sub) * SUB + h) * HD, HD)
            out_ref[:, pl.ds(at, HD)] = src[h]

    for sub in range(2):
        put(own_ref.at[sub], mine, sub)
        put(x_ref.at[sub], mine ^ 2, sub)
    put(za_ref, mine ^ 1, 0)
    put(da_ref, mine ^ 3, 0)
    put(zb_ref, mine ^ 1, 1)
    put(db_ref, mine ^ 3, 1)


def unpack(place, parts):
    return pl.pallas_call(
        unpack_kernel,
        out_shape=shape((BLK, HQ * HD), bf16),
        in_specs=[SMEM] + [VMEM] * 6,
        out_specs=VMEM,
        compiler_params=params(8),
        cost_estimate=pl.CostEstimate(flops=0, bytes_accessed=2 << 20, transcendentals=0),
        name="unpack",
    )(place, *parts)


def final_kernel(dkv_ref, tab, ks_ref, gk_ref, gv_ref, tq_ref, tk_ref):
    n = dkv_ref.shape[0]
    for head in range(HK):
        first = (head // 2) * (n // 2) + head % 2
        got = jnp.zeros((BLK + EXTRA, 2 * HD), f32)
        for i in range(first, first + n // 2, 2):
            got = got + dkv_ref[i].astype(f32)
        cols = slice(head * HD, (head + 1) * HD)
        g = unturn(got[:BLK, :HD].astype(bf16).astype(f32), tab[:, :HD], tab[:, HD:])
        gk_ref[:, cols] = (g * ks_ref[head : head + 1, :]).astype(bf16)
        gv_ref[:, cols] = got[:BLK, HD:].astype(bf16)
        term = got[BLK:, :HD] + got[BLK:, HD:]
        tq_ref[head * 2 * SUB : (head + 1) * 2 * SUB, :] = term[: 2 * SUB]
        tk_ref[head : head + 1, :] = term[2 * SUB : 2 * SUB + 1]


def final(dkv, table, ks):
    return pl.pallas_call(
        final_kernel,
        out_shape=(
            shape((BLK, HK * HD), bf16),
            shape((BLK, HK * HD), bf16),
            shape((HQ, HD), f32),
            shape((HK, HD), f32),
        ),
        in_specs=[VMEM] * 3,
        out_specs=(VMEM,) * 4,
        compiler_params=params(8),
        name="final",
    )(dkv, table, ks)


def shards(query, keys, values, grad_out, positions, q_scale, k_scale):
    n = lax.axis_size("seq")
    half = n // 2
    me = lax.axis_index("seq")
    x, z = me // half, me % half
    odd = z % 2
    kind = x * 2 + odd
    place = jnp.stack([kind, me]).astype(jnp.int32)
    za = z + 1 - 2 * odd
    zb = (z - 1 + 2 * odd) % half

    def pairs(flip, step):
        out = []
        for i in range(n):
            xi, zi = i // half, i % half
            zo = (zi + step * (1 - 2 * (zi % 2))) % half
            out.append((i, (xi ^ flip) * half + zo))
        return out

    def send(a, flip, step):
        return lax.ppermute(a, "seq", pairs(flip, step))

    kv = lax.all_to_all(pack_kv(keys[0], values[0], positions, n), "seq", 0, 0, tiled=True)
    own, to_x, to_za, to_da, to_zb, to_db = pack(place, query[0], grad_out[0])
    in_x = send(to_x, 1, 0)
    in_za, in_da = send(to_za, 0, 1), send(to_da, 1, 1)
    in_zb, in_db = send(to_zb, 0, -1), send(to_db, 1, -1)

    q_gain = lax.dynamic_slice_in_dim(q_scale.reshape(HK, 2 * SUB, HD), kind, 1, 0)[0]
    k_gain = lax.dynamic_slice_in_dim(k_scale.reshape(HK, HD), kind, 1, 0)
    keys_side = (kv, *prep(kv, angle_tables(), k_gain))
    sequences = lax.axis_size("dp")
    blocks = jnp.stack([me, me, me ^ half, me ^ half]).astype(jnp.int32)
    go, gx, *sums = attend(0, blocks, (own, in_x), *keys_side, q_gain, (), sequences)
    pair = lambda side: [side * half + za, side * half + zb]
    blocks = jnp.stack(pair(x) + pair(1 - x)).astype(jnp.int32)
    gza, gda, gzb, gdb, term, dkv = attend(
        1, blocks, (in_za, in_da, in_zb, in_db), *keys_side, q_gain, sums, sequences
    )

    term = lax.all_to_all(term, "dp", 0, 0, tiled=True)
    back = (go, send(gx, 1, 0), send(gza, 0, 1), send(gda, 1, 1), send(gzb, 0, -1), send(gdb, 1, -1))
    dkv, back = lax.optimization_barrier((add(term, dkv), back))
    dkv = lax.all_to_all(dkv, "seq", 0, 0, tiled=True)
    grad_query = unpack(place, back)
    grad_keys, grad_values, total_q, total_k = final(
        dkv, full_table(positions[0]), k_scale.reshape(HK, HD)
    )
    return (
        grad_query[None],
        grad_keys[None],
        grad_values[None],
        total_q.reshape(HQ * HD),
        total_k.reshape(HK * HD),
    )


def solution(mesh):
    return jax.shard_map(
        shards,
        mesh=mesh,
        in_specs=(
            P("dp", "seq", None),
            P("dp", "seq", None),
            P("dp", "seq", None),
            P("dp", "seq", None),
            P("dp", "seq"),
            P(),
            P(),
        ),
        out_specs=(P("dp", "seq", None), P("dp", "seq", None), P("dp", "seq", None), P(), P()),
        check_vma=False,
    )
```
